128 devices in a mesh: row: 8 (over z, core), col: 16 (over x, y).
Axes of the slice: x: 4, y: 4, z: 4, core: 2. Of those that a mesh axis runs over, the one named last changes fastest.
Arguments:
- aux_ints: bfloat16 [512, 1024, 1024], P(('row', 'col')), may hold values from -4 to 4
- density: bfloat16 [1024, 1024], P(('row', 'col')), may hold values from -0.1875 to 0.1875
- pattern: int32 [512, 8, 8], P(('row', 'col')), may hold values from 0 to 1, as said below
- block_sizes: int32 [8], replicated, may hold values from 96 to 128
Outputs:
- exchange_k: float32 [1024, 1024], P('row', 'col')
The draws below stay inside these ranges and needn't reach their ends.
Inputs may be any that keep to these rules, and one draw needn't show every extreme that they name: pattern[P, a, b] is 1 where both blocks a and b lie within a reach of the block of aux function P, else 0; every aux function has at least its own diagonal block.
All inputs are finite; a program needn't handle non-finite values.
Results may differ from the reference program's by a relative error of at most 0.0029.
Values may be sent and summed in bfloat16 or wider, within the bound.
No kernel may reach another device: no remote copies, remote signals or barrier semaphores. Data moves between devices by JAX's collectives and lax.ppermute only.
A program may use at most 128 MiB of HBM per device.

```python
import jax
import jax.numpy as jnp
from jax import lax

BS = 128
NB = 8
P_DEV = 4
N = 1024
NAUX = 512
DEVICES = 128


def draw_pattern(key, part):
    key = jax.random.fold_in(key, 11)
    key_center, key_spread, key_reach = jax.random.split(key, 3)
    center = jax.random.randint(key_center, (NAUX,), 0, NB)
    spread = jax.random.randint(key_spread, (DEVICES,), 1, NB + 1)
    spread_each = jnp.repeat(spread, P_DEV)
    reach = jax.random.randint(key_reach, (NAUX,), 0, spread_each)
    blocks = jnp.arange(NB, dtype=jnp.int32)
    near = jnp.abs(blocks[None, :] - center[:, None]) <= reach[:, None]
    return (near[:, :, None] & near[:, None, :]).astype(jnp.int32)


def set_ends(entries, stream_key, least, largest):
    extent = entries.shape
    place = [jax.random.randint(jax.random.fold_in(stream_key, axis), (), 0, extent[axis]) for axis in range(len(extent))]
    entries = entries.at[tuple(place)].set(least)
    longest = extent.index(max(extent))
    place[longest] = (place[longest] + 1) % extent[longest]
    return entries.at[tuple(place)].set(largest)


def spiked(array, stream_key, source, target, blocks, factor):
    def block_of(axis_at):
        return (jnp.arange(array.shape[axis_at]) // (array.shape[axis_at] // blocks)).reshape((-1,) + (1,) * (array.ndim - 1 - axis_at))

    first = jax.random.permutation(stream_key, blocks)[block_of(target)]
    far = (block_of(target) + blocks // 2) % blocks
    return jnp.where((block_of(source) == first) | (block_of(source) == far), factor * array, array)


def level_of(key, shape, cuts, smallest, largest):
    loudness = 1.0
    for position, shards_of in cuts:
        heights = jax.random.uniform(jax.random.fold_in(jax.random.fold_in(key, 6), position), (shards_of,), jnp.float32, smallest / len(cuts), largest / len(cuts))
        loudness = loudness * jnp.repeat(jnp.exp(heights), shape[position] // shards_of).reshape((-1,) + (1,) * (len(shape) - 1 - position))
    return loudness


def bell_draw(rng, shape, scale, most, cuts=(), held_as=jnp.bfloat16):
    result = scale * jax.random.normal(rng, shape, jnp.float32)
    if cuts:
        result = result * level_of(rng, shape, cuts, -0.22, 0.18)
    return jnp.clip(result, -most, most).astype(held_as)


def noise_with(rng, dims, scale, limit, pieces, heavy, kind=jnp.bfloat16):
    entries = scale * jax.random.normal(rng, dims, jnp.float32)
    if pieces:
        entries = entries * level_of(rng, dims, pieces, -0.22, 0.18)
    return jnp.clip(spiked(entries, jax.random.fold_in(rng, 3), *heavy), -limit, limit).astype(kind)


def setup_inputs(seed: int = 0) -> dict:
    splits = jax.random.split(jax.random.key(seed), 5)
    return {
        "aux_ints": noise_with(splits[0], (NAUX, N, N), (2.0 * (NAUX * N) ** -0.25), 4.0, ((0, 128),), (0, 1, 128, 5.5)),
        "density": bell_draw(splits[1], (N, N), N ** -0.5, 0.1875, ((0, 128),)),
        "pattern": draw_pattern(jax.random.fold_in(splits[4], 71), 0),
        "block_sizes": set_ends(jax.random.randint(splits[3], (NB,), BS * 3 // 4, BS + 1), jax.random.fold_in(splits[3], 1), BS * 3 // 4, BS).astype(jnp.int32),
    }


def mask_aux(aux_ints, pattern, block_sizes):
    aux_count, orbitals, _ = aux_ints.shape
    blocks = pattern.shape[1]
    block_width = orbitals // blocks
    inside = ((jnp.arange(orbitals, dtype=jnp.int32) % block_width) < jnp.repeat(block_sizes, block_width)).astype(aux_ints.dtype)
    shaped = aux_ints.reshape(aux_count, blocks, block_width, blocks, block_width)
    shaped = shaped * pattern[:, :, None, :, None].astype(aux_ints.dtype)
    return shaped.reshape(aux_count, orbitals, orbitals) * inside[None, :, None] * inside[None, None, :]


def reference(aux_ints, density, pattern, block_sizes):
    orbitals = aux_ints.shape[1]

    def one_aux(total, pair):
        slab, marks = pair
        masked = mask_aux(slab[None], marks[None], block_sizes)[0]
        coeff = jnp.dot(masked, density, preferred_element_type=jnp.float32).astype(jnp.bfloat16)
        return total + jnp.dot(coeff, masked.T, preferred_element_type=jnp.float32), None

    total, _ = lax.scan(one_aux, jnp.zeros((orbitals, orbitals), jnp.float32), (aux_ints, pattern))
    return total
```

```python
import functools

import jax
import jax.numpy as jnp
from jax import lax
from jax.experimental import pallas as pl
from jax.experimental.pallas import tpu as pltpu
from jax.sharding import Mesh, PartitionSpec as P

F32 = jnp.float32
BF16 = jnp.bfloat16
BS = 128
NB = 8
N = BS * NB
P_DEV = 4
HALF = N // 2
TILE = 256
NN = (((1,), (0,)), ((), ()))
NT = (((1,), (1,)), ((), ()))
CHIPS = ("z", "x", "y")


def column_mask(sizes_ref):
    lane = lax.broadcasted_iota(jnp.int32, (1, BS), 1)
    return jnp.concatenate([(lane < sizes_ref[b]).astype(F32) for b in range(NB)], axis=1)


def partial_kernel(place_ref, sizes_ref, pattern_ref, aux_hbm, mine_ref, theirs_ref, out_ref, dens, aux, coeff, sems):
    core, side = place_ref[0], place_ref[1]
    copies = [pltpu.make_async_copy(aux_hbm.at[p], aux.at[p], sems.at[p]) for p in range(P_DEV)]
    for copy in copies:
        copy.start()

    cols = column_mask(sizes_ref)
    row = lax.broadcasted_iota(jnp.int32, (BS, 1), 0)
    for z in range(NB // 2):
        for half_ref, c in ((mine_ref, core), (theirs_ref, 1 - core)):
            b = 2 * z + c
            keep = (row < sizes_ref[b]).astype(F32) * cols
            start = pl.multiple_of(b * BS, BS)
            dens[pl.ds(start, BS), :] = half_ref[z * BS:(z + 1) * BS, :] * keep.astype(BF16)

    for p in range(P_DEV):
        copies[p].wait()
        near = [pattern_ref[p, b, b] for b in range(NB)]
        count = functools.reduce(lambda a, b: a + b, near)

        @pl.when(count < NB)
        def _():
            ones = jnp.ones((1, BS), F32)
            wide = jnp.concatenate([ones * w.astype(F32) for w in near], axis=1)
            for b in range(NB):
                factor = (wide * near[b].astype(F32)).astype(BF16)
                aux[p, b * BS:(b + 1) * BS, :] = aux[p, b * BS:(b + 1) * BS, :] * factor

        rows = jnp.concatenate(
            [aux[p, pl.ds(pl.multiple_of((2 * z + side) * BS, BS), BS), :] for z in range(NB // 2)], axis=0
        )
        for t in range(N // TILE):
            s = slice(t * TILE, (t + 1) * TILE)
            coeff[p, :, s] = lax.dot_general(rows, dens[:, s], NN, preferred_element_type=F32).astype(BF16)

    for t in range(HALF // TILE):
        s = slice(t * TILE, (t + 1) * TILE)
        total = lax.dot_general(aux[0], coeff[0, s, :], NT, preferred_element_type=F32)
        for p in range(1, P_DEV):
            total += lax.dot_general(aux[p], coeff[p, s, :], NT, preferred_element_type=F32)
        for h in range(TILE // BS):
            out_ref[t * (TILE // BS) + h] = total[:, h * BS:(h + 1) * BS]


def partial_sums(place, sizes, pattern, aux_ints, mine, theirs):
    smem = pl.BlockSpec(memory_space=pltpu.SMEM)
    vmem = pl.BlockSpec(memory_space=pltpu.VMEM)
    return pl.pallas_call(
        partial_kernel,
        in_specs=[smem, smem, smem, pl.BlockSpec(memory_space=pl.ANY), vmem, vmem],
        out_specs=vmem,
        out_shape=jax.ShapeDtypeStruct((NB // 2, N, BS), F32),
        scratch_shapes=[
            pltpu.VMEM((N, N), BF16),
            pltpu.VMEM((P_DEV, N, N), BF16),
            pltpu.VMEM((P_DEV, HALF, N), BF16),
            pltpu.SemaphoreType.DMA((P_DEV,)),
        ],
        compiler_params=pltpu.CompilerParams(vmem_limit_bytes=40 * 2**20),
        cost_estimate=pl.CostEstimate(flops=P_DEV * 2 * N * N * N, bytes_accessed=2 * P_DEV * N * N, transcendentals=0),
    )(place, sizes, pattern, aux_ints, mine, theirs)


def finish_kernel(place_ref, sizes_ref, parts_ref, out_ref):
    total = jnp.sum(parts_ref[...].astype(F32), axis=0)
    mu = lax.broadcasted_iota(jnp.int32, (BS // 2, BS), 1)
    nu = lax.broadcasted_iota(jnp.int32, (BS // 2, BS), 0)
    xy = place_ref[1]
    nu = nu + (xy % 2) * (BS // 2)
    keep = (mu < sizes_ref[place_ref[0]]) & (nu < sizes_ref[xy // 2])
    out_ref[...] = jnp.where(keep, total, 0.0).T


def finish(place, sizes, parts):
    smem = pl.BlockSpec(memory_space=pltpu.SMEM)
    vmem = pl.BlockSpec(memory_space=pltpu.VMEM)
    return pl.pallas_call(
        finish_kernel,
        in_specs=[smem, smem, vmem],
        out_specs=vmem,
        out_shape=jax.ShapeDtypeStruct((BS, BS // 2), F32),
        compiler_params=pltpu.CompilerParams(vmem_limit_bytes=16 * 2**20),
    )(place, sizes, parts)


def local(aux_ints, density, pattern, block_sizes):
    z, c, x, y = (lax.axis_index(a) for a in ("z", "c", "x", "y"))
    swap = [(0, 1), (1, 0)]
    spread = jnp.broadcast_to(density[None], (64, 8, N))
    mine = lax.all_to_all(spread, CHIPS, 0, 0).reshape(HALF, N)
    theirs = lax.ppermute(mine, "c", swap)
    send = partial_sums(jnp.stack([c, 1 - c]), block_sizes, pattern, aux_ints, mine, theirs)
    got = lax.ppermute(send, "c", swap)
    keep = partial_sums(jnp.stack([c, c]), block_sizes, pattern, aux_ints, mine, theirs)
    chip = (keep + got).astype(BF16).reshape(64, BS // 2, BS)
    parts = lax.all_to_all(chip, CHIPS, 0, 0)
    return finish(jnp.stack([2 * z + c, 4 * x + y]), block_sizes, parts)


def solution(mesh):
    whole = Mesh(mesh.devices.reshape(4, 2, 4, 4), ("z", "c", "x", "y"))
    everywhere = ("z", "c", "x", "y")
    in_specs = (P(everywhere, None, None), P(everywhere, None), P(everywhere, None, None), P())
    return jax.shard_map(local, mesh=whole, in_specs=in_specs, out_specs=P(("z", "c"), ("x", "y")), check_vma=False)
```

```python
import jax
import jax.numpy as jnp
from jax import lax
from jax.experimental import pallas as pl
from jax.experimental.pallas import tpu as pltpu
from jax.sharding import Mesh, PartitionSpec as P

F32 = jnp.float32
BF16 = jnp.bfloat16
BS = 128
NB = 8
N = BS * NB
P_DEV = 4
WIDE = P_DEV * N
HALF = N // 2
TILE = 256
PIECES = 4
AHEAD = 4
CHIP_COUNT = 64
ROWS = 8
NN = (((1,), (0,)), ((), ()))
NT = (((1,), (1,)), ((), ()))
CHIPS = ("z", "x", "y")
SMEM = pl.BlockSpec(memory_space=pltpu.SMEM)
HBM = pl.BlockSpec(memory_space=pltpu.HBM)
VMEM = pl.BlockSpec(memory_space=pltpu.VMEM)


def params(mib):
    return pltpu.CompilerParams(vmem_limit_bytes=mib * 2**20)


def prepare_kernel(sizes, pattern, aux, out):
    p = pl.program_id(0)
    lane = lax.broadcasted_iota(jnp.int32, (1, BS), 1)
    row = lax.broadcasted_iota(jnp.int32, (BS, 1), 0)
    near = [pattern[p, b, b] for b in range(NB)]
    cols = jnp.concatenate([((lane < sizes[b]) & (near[b] > 0)).astype(F32) for b in range(NB)], axis=1)
    for b in range(NB):
        rows = ((row < sizes[b]) & (near[b] > 0)).astype(F32)
        at = slice(b * BS, (b + 1) * BS)
        out[at, :] = aux[0, at, :] * (rows * cols).astype(BF16)


def prepare(sizes, pattern, aux):
    return pl.pallas_call(
        prepare_kernel,
        grid=(P_DEV,),
        in_specs=[SMEM, SMEM, pl.BlockSpec((1, N, N), lambda p: (p, 0, 0))],
        out_specs=pl.BlockSpec((N, N), lambda p: (0, p)),
        out_shape=pltpu.HBM((N, WIDE), BF16),
        compiler_params=params(48),
        cost_estimate=pl.CostEstimate(flops=0, bytes_accessed=2 * 2 * N * WIDE, transcendentals=0),
    )(sizes, pattern, aux)


def block(index):
    return pl.ds(pl.multiple_of(index * BS, BS), BS)


def gather_rows(p, side, order, aux):
    return jnp.concatenate(
        [
            jnp.concatenate([aux[block(2 * z + side), block(p * NB + k)] for k in order], axis=1)
            for z in range(NB // 2)
        ],
        axis=0,
    )


def blocks_of(core):
    return [2 * z + core for z in range(NB // 2)]


def tiles(p):
    for t in range(N // TILE):
        yield slice(t * TILE, (t + 1) * TILE), slice(p * N + t * TILE, p * N + (t + 1) * TILE)


def half_sums(aux, coeff, store):
    for t in range(HALF // TILE):
        value = lax.dot_general(aux[...], coeff[t * TILE:(t + 1) * TILE, :], NT, preferred_element_type=F32)
        for h in range(TILE // BS):
            store(t * (TILE // BS) + h, value[:, h * BS:(h + 1) * BS])


def first_kernel(place, aux_hbm, mine, part, aux, sems):
    depth = N // PIECES

    def copies(p):
        pieces = []
        for i in range(PIECES):
            at = (slice(i * depth, (i + 1) * depth), slice(p * N, (p + 1) * N))
            pieces.append(pltpu.make_async_copy(aux_hbm.at[at], aux.at[at], sems.at[p, i]))
        return pieces

    for p in range(AHEAD):
        for copy in copies(p):
            copy.start()
    for p in range(P_DEV):
        for copy in copies(p):
            copy.wait()
        if p + AHEAD < P_DEV:
            for copy in copies(p + AHEAD):
                copy.start()
        rows = gather_rows(p, 1 - place[1], blocks_of(place[1]), aux)
        for s, at in tiles(p):
            part[:, at] = lax.dot_general(rows, mine[:, s], NN, preferred_element_type=F32)


def first_part(place, aux, mine):
    return pl.pallas_call(
        first_kernel,
        in_specs=[SMEM, HBM, VMEM],
        out_specs=[VMEM, VMEM],
        out_shape=[jax.ShapeDtypeStruct((HALF, WIDE), F32), jax.ShapeDtypeStruct((N, WIDE), BF16)],
        scratch_shapes=[pltpu.SemaphoreType.DMA((P_DEV, PIECES))],
        compiler_params=params(30),
        cost_estimate=pl.CostEstimate(flops=N * N * WIDE // 2, bytes_accessed=0, transcendentals=0),
    )(place, aux, mine)


def send_kernel(place, aux, theirs, part, out, coeff):
    for p in range(P_DEV):
        rows = gather_rows(p, 1 - place[1], blocks_of(1 - place[1]), aux)
        for s, at in tiles(p):
            value = lax.dot_general(rows, theirs[:, s], NN, preferred_element_type=F32)
            coeff[:, at] = (part[:, at] + value).astype(BF16)

    def store(z, value):
        out[z] = value

    half_sums(aux, coeff, store)


def send_sums(place, aux, theirs, part):
    return pl.pallas_call(
        send_kernel,
        in_specs=[SMEM, VMEM, VMEM, VMEM],
        out_specs=VMEM,
        out_shape=jax.ShapeDtypeStruct((NB // 2, N, BS), F32),
        scratch_shapes=[pltpu.VMEM((HALF, WIDE), BF16)],
        compiler_params=params(20),
        cost_estimate=pl.CostEstimate(flops=3 * N * N * WIDE // 2, bytes_accessed=0, transcendentals=0),
    )(place, aux, theirs, part)


def keep_coeff_kernel(place, aux, mine, theirs, coeff):
    order = blocks_of(place[1]) + blocks_of(1 - place[1])
    for p in range(P_DEV):
        rows = gather_rows(p, place[1], order, aux)
        for s, at in tiles(p):
            dens = jnp.concatenate([mine[:, s], theirs[:, s]], axis=0)
            coeff[:, at] = lax.dot_general(rows, dens, NN, preferred_element_type=F32).astype(BF16)


def keep_coeff(place, aux, mine, theirs):
    return pl.pallas_call(
        keep_coeff_kernel,
        in_specs=[SMEM, VMEM, VMEM, VMEM],
        out_specs=VMEM,
        out_shape=jax.ShapeDtypeStruct((HALF, WIDE), BF16),
        compiler_params=params(20),
        cost_estimate=pl.CostEstimate(flops=N * N * WIDE, bytes_accessed=0, transcendentals=0),
    )(place, aux, mine, theirs)


def keep_sums_kernel(aux, coeff, got, out):
    def store(z, value):
        out[z] = (value + got[z]).astype(BF16)

    half_sums(aux, coeff, store)


def keep_sums(aux, coeff, got):
    return pl.pallas_call(
        keep_sums_kernel,
        in_specs=[VMEM, VMEM, VMEM],
        out_specs=VMEM,
        out_shape=jax.ShapeDtypeStruct((NB // 2, N, BS), BF16),
        compiler_params=params(20),
        cost_estimate=pl.CostEstimate(flops=N * N * WIDE, bytes_accessed=0, transcendentals=0),
    )(aux, coeff, got)


def finish_kernel(parts, out):
    out[...] = jnp.sum(parts[...].astype(F32), axis=0)


def finish(parts):
    return pl.pallas_call(
        finish_kernel,
        in_specs=[VMEM],
        out_specs=VMEM,
        out_shape=jax.ShapeDtypeStruct((BS // 2, BS), F32),
        compiler_params=params(16),
    )(parts)


def local(aux_ints, density, pattern, block_sizes):
    place = jnp.stack([lax.axis_index("z"), lax.axis_index("c")])
    swap = [(0, 1), (1, 0)]
    everyone = jnp.broadcast_to(density[None], (CHIP_COUNT, ROWS, N))
    mine = lax.all_to_all(everyone, CHIPS, 0, 0).reshape(HALF, N)
    mine, masked = lax.optimization_barrier((mine, prepare(block_sizes, pattern, aux_ints)))
    theirs = lax.ppermute(mine, "c", swap)
    part, aux = first_part(place, masked, mine)
    got = lax.ppermute(send_sums(place, aux, theirs, part), "c", swap)
    chip = keep_sums(aux, keep_coeff(place, aux, mine, theirs), got)
    parts = lax.all_to_all(chip.reshape(CHIP_COUNT, BS // 2, BS), CHIPS, 0, 0)
    return finish(parts).T


def solution(mesh):
    whole = Mesh(mesh.devices.reshape(4, 2, 4, 4), ("z", "c", "x", "y"))
    everywhere = ("z", "c", "x", "y")
    in_specs = (P(everywhere, None, None), P(everywhere, None), P(everywhere, None, None), P())
    return jax.shard_map(local, mesh=whole, in_specs=in_specs, out_specs=P(("z", "c"), ("x", "y")), check_vma=False)
```

```python
import jax
import jax.numpy as jnp
from jax import lax
from jax.experimental import pallas as pl
from jax.experimental.pallas import tpu as pltpu
from jax.sharding import Mesh, PartitionSpec as P

F32 = jnp.float32
BF16 = jnp.bfloat16
BS = 128
NB = 8
N = BS * NB
P_DEV = 4
WIDE = P_DEV * N
HALF = N // 2
TILE = 256
CHIP_COUNT = 64
ROWS = 8
NN = (((1,), (0,)), ((), ()))
NT = (((1,), (1,)), ((), ()))
CHIPS = ("z", "x", "y")
SMEM = pl.BlockSpec(memory_space=pltpu.SMEM)
VMEM = pl.BlockSpec(memory_space=pltpu.VMEM)


def params(mib):
    return pltpu.CompilerParams(vmem_limit_bytes=mib * 2**20)


def cost(products):
    return pl.CostEstimate(flops=int(products * N * N * WIDE), bytes_accessed=0, transcendentals=0)


def core_order(core):
    return [2 * z + core for z in range(NB // 2)] + [2 * z + 1 - core for z in range(NB // 2)]


def block(index):
    return pl.ds(pl.multiple_of(index * BS, BS), BS)


def prepare_kernel(place, sizes, pattern, aux, send_own, send_other, keep_own, keep_other):
    p = pl.program_id(0)
    lane = lax.broadcasted_iota(jnp.int32, (1, BS), 1)
    row = lax.broadcasted_iota(jnp.int32, (BS, 1), 0)
    order = core_order(place[0])
    cols = [((lane < sizes[b]) & (pattern[p, b, b] > 0)).astype(F32) for b in order]
    outs = ((keep_own, keep_other), (send_own, send_other))
    for i, b in enumerate(order):
        rows = ((row < sizes[b]) & (pattern[p, b, b] > 0)).astype(F32)
        half, at = divmod(i, NB // 2)
        for j, k in enumerate(order):
            value = aux[0, block(b), block(k)] * (rows * cols[j]).astype(BF16)
            other, to = divmod(j, NB // 2)
            outs[half][other][at * BS:(at + 1) * BS, to * BS:(to + 1) * BS] = value


def prepare(place, sizes, pattern, aux):
    quarter = pl.BlockSpec((HALF, HALF), lambda p: (0, p))
    return pl.pallas_call(
        prepare_kernel,
        grid=(P_DEV,),
        in_specs=[SMEM, SMEM, SMEM, pl.BlockSpec((1, N, N), lambda p: (p, 0, 0))],
        out_specs=[quarter] * 4,
        out_shape=[pltpu.HBM((HALF, WIDE // 2), BF16)] * 4,
        compiler_params=params(48),
        cost_estimate=pl.CostEstimate(flops=0, bytes_accessed=2 * 2 * N * WIDE, transcendentals=0),
    )(place, sizes, pattern, aux)


def tiles(p):
    for t in range(N // TILE):
        other, within = divmod(t * TILE, HALF)
        swapped = (1 - other) * HALF + within
        at = other * (WIDE // 2) + p * HALF + within
        yield slice(t * TILE, (t + 1) * TILE), slice(swapped, swapped + TILE), slice(at, at + TILE)


def slab(p):
    return slice(p * HALF, (p + 1) * HALF)


def first_kernel(send_own, mine, part):
    for p in range(P_DEV):
        for s, _, at in tiles(p):
            part[:, at] = lax.dot_general(send_own[:, slab(p)], mine[:, s], NN, preferred_element_type=F32)


def first_part(send_own, mine):
    return pl.pallas_call(
        first_kernel,
        in_specs=[VMEM, VMEM],
        out_specs=VMEM,
        out_shape=jax.ShapeDtypeStruct((HALF, WIDE), F32),
        compiler_params=params(20),
        cost_estimate=cost(0.5),
    )(send_own, mine)


def half_sums(aux, coeff, store):
    send_own, send_other, keep_own, keep_other = aux
    rows = jnp.concatenate(
        [
            jnp.concatenate([send_own[...], send_other[...]], axis=1),
            jnp.concatenate([keep_own[...], keep_other[...]], axis=1),
        ],
        axis=0,
    )
    for t in range(HALF // TILE):
        value = lax.dot_general(rows, coeff[t * TILE:(t + 1) * TILE, :], NT, preferred_element_type=F32)
        for h in range(TILE // BS):
            store(t * (TILE // BS) + h, value[:, h * BS:(h + 1) * BS])


def send_kernel(send_own, send_other, keep_own, keep_other, theirs, part, out, coeff):
    for p in range(P_DEV):
        for s, swapped, at in tiles(p):
            value = lax.dot_general(send_other[:, slab(p)], theirs[:, swapped], NN, preferred_element_type=F32)
            coeff[:, at] = (part[:, at] + value).astype(BF16)

    def store(z, value):
        out[z] = value

    half_sums((send_own, send_other, keep_own, keep_other), coeff, store)


def send_sums(aux, theirs, part):
    return pl.pallas_call(
        send_kernel,
        in_specs=[VMEM] * 6,
        out_specs=VMEM,
        out_shape=jax.ShapeDtypeStruct((NB // 2, N, BS), F32),
        scratch_shapes=[pltpu.VMEM((HALF, WIDE), BF16)],
        compiler_params=params(20),
        cost_estimate=cost(1.5),
    )(*aux, theirs, part)


def keep_coeff_kernel(keep_own, keep_other, mine, theirs, coeff):
    for p in range(P_DEV):
        rows = jnp.concatenate([keep_own[:, slab(p)], keep_other[:, slab(p)]], axis=1)
        for s, swapped, at in tiles(p):
            dens = jnp.concatenate([mine[:, s], theirs[:, swapped]], axis=0)
            coeff[:, at] = lax.dot_general(rows, dens, NN, preferred_element_type=F32).astype(BF16)


def keep_coeff(aux, mine, theirs):
    return pl.pallas_call(
        keep_coeff_kernel,
        in_specs=[VMEM] * 4,
        out_specs=VMEM,
        out_shape=jax.ShapeDtypeStruct((HALF, WIDE), BF16),
        compiler_params=params(20),
        cost_estimate=cost(1),
    )(aux[2], aux[3], mine, theirs)


def keep_sums_kernel(send_own, send_other, keep_own, keep_other, coeff, got, out):
    def store(z, value):
        out[z] = (value + jnp.concatenate([got[z, HALF:, :], got[z, :HALF, :]], axis=0)).astype(BF16)

    half_sums((send_own, send_other, keep_own, keep_other), coeff, store)


def keep_sums(aux, coeff, got):
    return pl.pallas_call(
        keep_sums_kernel,
        in_specs=[VMEM] * 6,
        out_specs=VMEM,
        out_shape=jax.ShapeDtypeStruct((NB // 2, N, BS), BF16),
        compiler_params=params(20),
        cost_estimate=cost(1),
    )(*aux, coeff, got)


def finish_kernel(parts, out):
    out[...] = jnp.sum(parts[...].astype(F32), axis=0)


def finish(parts):
    return pl.pallas_call(
        finish_kernel,
        in_specs=[VMEM],
        out_specs=VMEM,
        out_shape=jax.ShapeDtypeStruct((BS // 2, BS), F32),
        compiler_params=params(16),
    )(parts)


def sums_groups():
    return [
        [(z * 2 + core) * 16 + 2 * b + h for z in range(NB // 2) for b in core_order(1 - core) for h in range(2)]
        for core in range(2)
    ]


def local(aux_ints, density, pattern, block_sizes):
    core = lax.axis_index("c")
    swap = [(0, 1), (1, 0)]
    blocks = density.reshape(ROWS, NB // 2, 2, BS).swapaxes(1, 2)
    blocks = jnp.where(core == 0, blocks, blocks[:, ::-1]).reshape(ROWS, N)
    everyone = jnp.broadcast_to(blocks[None], (CHIP_COUNT, ROWS, N))
    mine = lax.all_to_all(everyone, CHIPS, 0, 0).reshape(HALF, N)
    mine, aux = lax.optimization_barrier((mine, prepare(core[None], block_sizes, pattern, aux_ints)))
    theirs = lax.ppermute(mine, "c", swap)
    part = first_part(aux[0], mine)
    got = lax.ppermute(send_sums(aux, theirs, part), "c", swap)
    chip = keep_sums(aux, keep_coeff(aux, mine, theirs), got)
    chip = chip.reshape(CHIP_COUNT, BS // 2, BS)
    parts = lax.all_to_all(chip, ("z", "c", "x", "y"), 0, 0, axis_index_groups=sums_groups())
    return finish(parts).T


def solution(mesh):
    whole = Mesh(mesh.devices.reshape(4, 2, 4, 4), ("z", "c", "x", "y"))
    everywhere = ("z", "c", "x", "y")
    in_specs = (P(everywhere, None, None), P(everywhere, None), P(everywhere, None, None), P())
    return jax.shard_map(local, mesh=whole, in_specs=in_specs, out_specs=P(("z", "c"), ("x", "y")), check_vma=False)
```

```python
import jax
import jax.numpy as jnp
from jax import lax
from jax.experimental import pallas as pl
from jax.experimental.pallas import tpu as pltpu
from jax.sharding import Mesh, PartitionSpec as P

F32 = jnp.float32
BF16 = jnp.bfloat16
BS = 128
NB = 8
N = BS * NB
P_DEV = 4
WIDE = P_DEV * N
HALF = N // 2
TILE = 256
CHIP_COUNT = 64
ROWS = 8
NN = (((1,), (0,)), ((), ()))
NT = (((1,), (1,)), ((), ()))
CHIPS = ("z", "x", "y")
SMEM = pl.BlockSpec(memory_space=pltpu.SMEM)
VMEM = pl.BlockSpec(memory_space=pltpu.VMEM)


def params(mib):
    return pltpu.CompilerParams(vmem_limit_bytes=mib * 2**20)


def cost(products):
    return pl.CostEstimate(flops=int(products * N * N * WIDE), bytes_accessed=0, transcendentals=0)


def core_order(core):
    return [2 * z + core for z in range(NB // 2)] + [2 * z + 1 - core for z in range(NB // 2)]


def block(index):
    return pl.ds(pl.multiple_of(index * BS, BS), BS)


def prepare_kernel(place, sizes, pattern, aux, send_own, send_other, keep_own, keep_other):
    p = pl.program_id(0)
    lane = lax.broadcasted_iota(jnp.int32, (1, BS), 1)
    row = lax.broadcasted_iota(jnp.int32, (BS, 1), 0)
    order = core_order(place[0])
    cols = [((lane < sizes[b]) & (pattern[p, b, b] > 0)).astype(F32) for b in order]
    outs = ((keep_own, keep_other), (send_own, send_other))
    for i, b in enumerate(order):
        rows = ((row < sizes[b]) & (pattern[p, b, b] > 0)).astype(F32)
        half, at = divmod(i, NB // 2)
        for j, k in enumerate(order):
            value = aux[0, block(b), block(k)] * (rows * cols[j]).astype(BF16)
            other, to = divmod(j, NB // 2)
            which = p if half and not other else 0
            outs[half][other][which, at * BS:(at + 1) * BS, to * BS:(to + 1) * BS] = value


def prepare(place, sizes, pattern, aux):
    quarter = pl.BlockSpec((1, HALF, HALF), lambda p: (p, 0, 0))
    return pl.pallas_call(
        prepare_kernel,
        grid=(P_DEV,),
        in_specs=[SMEM, SMEM, SMEM, pl.BlockSpec((1, N, N), lambda p: (p, 0, 0))],
        out_specs=[VMEM] + [quarter] * 3,
        out_shape=[jax.ShapeDtypeStruct((P_DEV, HALF, HALF), BF16)] + [pltpu.HBM((P_DEV, HALF, HALF), BF16)] * 3,
        compiler_params=params(48),
        cost_estimate=pl.CostEstimate(flops=0, bytes_accessed=2 * 2 * N * WIDE, transcendentals=0),
    )(place, sizes, pattern, aux)


def tiles(p):
    for t in range(N // TILE):
        other, within = divmod(t * TILE, HALF)
        swapped = (1 - other) * HALF + within
        at = other * (WIDE // 2) + p * HALF + within
        yield slice(t * TILE, (t + 1) * TILE), slice(swapped, swapped + TILE), slice(at, at + TILE)


def first_kernel(send_own, mine, part):
    for p in range(P_DEV):
        for s, _, at in tiles(p):
            part[:, at] = lax.dot_general(send_own[p], mine[:, s], NN, preferred_element_type=F32)


def first_part(send_own, mine):
    return pl.pallas_call(
        first_kernel,
        in_specs=[VMEM, VMEM],
        out_specs=VMEM,
        out_shape=jax.ShapeDtypeStruct((HALF, WIDE), F32),
        compiler_params=params(20),
        cost_estimate=cost(0.5),
    )(send_own, mine)


def half_sums(aux, coeff, store):
    send_own, send_other, keep_own, keep_other = aux
    rows = jnp.concatenate(
        [
            jnp.concatenate([quarter[p] for quarter in half for p in range(P_DEV)], axis=1)
            for half in ((send_own, send_other), (keep_own, keep_other))
        ],
        axis=0,
    )
    for t in range(HALF // TILE):
        value = lax.dot_general(rows, coeff[t * TILE:(t + 1) * TILE, :], NT, preferred_element_type=F32)
        for h in range(TILE // BS):
            store(t * (TILE // BS) + h, value[:, h * BS:(h + 1) * BS])


def send_kernel(send_own, send_other, keep_own, keep_other, theirs, part, out, coeff):
    for p in range(P_DEV):
        for s, swapped, at in tiles(p):
            value = lax.dot_general(send_other[p], theirs[:, swapped], NN, preferred_element_type=F32)
            coeff[:, at] = (part[:, at] + value).astype(BF16)

    def store(z, value):
        out[z] = value

    half_sums((send_own, send_other, keep_own, keep_other), coeff, store)


def send_sums(aux, theirs, part):
    return pl.pallas_call(
        send_kernel,
        in_specs=[VMEM] * 6,
        out_specs=VMEM,
        out_shape=jax.ShapeDtypeStruct((NB // 2, N, BS), F32),
        scratch_shapes=[pltpu.VMEM((HALF, WIDE), BF16)],
        compiler_params=params(20),
        cost_estimate=cost(1.5),
    )(*aux, theirs, part)


def keep_coeff_kernel(keep_own, keep_other, mine, theirs, coeff):
    for p in range(P_DEV):
        rows = jnp.concatenate([keep_own[p], keep_other[p]], axis=1)
        for s, swapped, at in tiles(p):
            dens = jnp.concatenate([mine[:, s], theirs[:, swapped]], axis=0)
            coeff[:, at] = lax.dot_general(rows, dens, NN, preferred_element_type=F32).astype(BF16)


def keep_coeff(aux, mine, theirs):
    return pl.pallas_call(
        keep_coeff_kernel,
        in_specs=[VMEM] * 4,
        out_specs=VMEM,
        out_shape=jax.ShapeDtypeStruct((HALF, WIDE), BF16),
        compiler_params=params(20),
        cost_estimate=cost(1),
    )(aux[2], aux[3], mine, theirs)


def keep_sums_kernel(send_own, send_other, keep_own, keep_other, coeff, got, out):
    def store(z, value):
        out[z] = (value + jnp.concatenate([got[z, HALF:, :], got[z, :HALF, :]], axis=0)).astype(BF16)

    half_sums((send_own, send_other, keep_own, keep_other), coeff, store)


def keep_sums(aux, coeff, got):
    return pl.pallas_call(
        keep_sums_kernel,
        in_specs=[VMEM] * 6,
        out_specs=VMEM,
        out_shape=jax.ShapeDtypeStruct((NB // 2, N, BS), BF16),
        compiler_params=params(20),
        cost_estimate=cost(1),
    )(*aux, coeff, got)


def finish_kernel(parts, out):
    out[...] = jnp.sum(parts[...].astype(F32), axis=0)


def finish(parts):
    return pl.pallas_call(
        finish_kernel,
        in_specs=[VMEM],
        out_specs=VMEM,
        out_shape=jax.ShapeDtypeStruct((BS // 2, BS), F32),
        compiler_params=params(16),
    )(parts)


def sums_groups():
    return [
        [(z * 2 + core) * 16 + 2 * b + h for z in range(NB // 2) for b in core_order(1 - core) for h in range(2)]
        for core in range(2)
    ]


def local(aux_ints, density, pattern, block_sizes):
    core = lax.axis_index("c")
    swap = [(0, 1), (1, 0)]
    blocks = density.reshape(ROWS, NB // 2, 2, BS).swapaxes(1, 2)
    blocks = jnp.where(core == 0, blocks, blocks[:, ::-1]).reshape(ROWS, N)
    everyone = jnp.broadcast_to(blocks[None], (CHIP_COUNT, ROWS, N))
    mine = lax.all_to_all(everyone, CHIPS, 0, 0).reshape(HALF, N)
    mine, aux = lax.optimization_barrier((mine, prepare(core[None], block_sizes, pattern, aux_ints)))
    theirs = lax.ppermute(mine, "c", swap)
    part = first_part(aux[0], mine)
    got = lax.ppermute(send_sums(aux, theirs, part), "c", swap)
    chip = keep_sums(aux, keep_coeff(aux, mine, theirs), got)
    chip = chip.reshape(CHIP_COUNT, BS // 2, BS)
    parts = lax.all_to_all(chip, ("z", "c", "x", "y"), 0, 0, axis_index_groups=sums_groups())
    return finish(parts).T


def solution(mesh):
    whole = Mesh(mesh.devices.reshape(4, 2, 4, 4), ("z", "c", "x", "y"))
    everywhere = ("z", "c", "x", "y")
    in_specs = (P(everywhere, None, None), P(everywhere, None), P(everywhere, None, None), P())
    return jax.shard_map(local, mesh=whole, in_specs=in_specs, out_specs=P(("z", "c"), ("x", "y")), check_vma=False)
```

```python
import functools

import jax
import jax.numpy as jnp
from jax import lax
from jax.experimental import pallas as pl
from jax.experimental.pallas import tpu as pltpu
from jax.sharding import Mesh, PartitionSpec as P

F32 = jnp.float32
BF16 = jnp.bfloat16
BS = 128
NB = 8
N = BS * NB
P_DEV = 4
WIDE = P_DEV * N
HALF = N // 2
TILE = 256
CHIP_COUNT = 64
ROWS = 8
NN = (((1,), (0,)), ((), ()))
NT = (((1,), (1,)), ((), ()))
CHIPS = ("z", "x", "y")
SMEM = pl.BlockSpec(memory_space=pltpu.SMEM)
VMEM = pl.BlockSpec(memory_space=pltpu.VMEM)


def params(mib):
    return pltpu.CompilerParams(vmem_limit_bytes=mib * 2**20)


def cost(products):
    return pl.CostEstimate(flops=int(products * N * N * WIDE), bytes_accessed=0, transcendentals=0)


def core_order(core):
    return [2 * z + core for z in range(NB // 2)] + [2 * z + 1 - core for z in range(NB // 2)]


def row_order(core, odd):
    zs = (1 - odd, 3 - odd, odd, odd + 2)
    return [2 * z + core for z in zs] + [2 * z + 1 - core for z in zs]


def block(index):
    return pl.ds(pl.multiple_of(index * BS, BS), BS)


def prepare_kernel(place, sizes, pattern, aux, send_own, send_other, keep_own, keep_other):
    p = pl.program_id(0)
    lane = lax.broadcasted_iota(jnp.int32, (1, BS), 1)
    row = lax.broadcasted_iota(jnp.int32, (BS, 1), 0)
    order = core_order(place[0])
    rows_order = row_order(place[0], place[1])
    cols = [((lane < sizes[b]) & (pattern[p, b, b] > 0)).astype(F32) for b in order]
    outs = ((keep_own, keep_other), (send_own, send_other))
    for i, b in enumerate(rows_order):
        rows = ((row < sizes[b]) & (pattern[p, b, b] > 0)).astype(F32)
        half, at = divmod(i, NB // 2)
        for j, k in enumerate(order):
            value = aux[0, block(b), block(k)] * (rows * cols[j]).astype(BF16)
            other, to = divmod(j, NB // 2)
            which = p if half and not other else 0
            outs[half][other][which, at * BS:(at + 1) * BS, to * BS:(to + 1) * BS] = value


def prepare(place, sizes, pattern, aux):
    quarter = pl.BlockSpec((1, HALF, HALF), lambda p: (p, 0, 0))
    return pl.pallas_call(
        prepare_kernel,
        grid=(P_DEV,),
        in_specs=[SMEM, SMEM, SMEM, pl.BlockSpec((1, N, N), lambda p: (p, 0, 0))],
        out_specs=[VMEM] + [quarter] * 3,
        out_shape=[jax.ShapeDtypeStruct((P_DEV, HALF, HALF), BF16)] + [pltpu.HBM((P_DEV, HALF, HALF), BF16)] * 3,
        compiler_params=params(48),
        cost_estimate=pl.CostEstimate(flops=0, bytes_accessed=2 * 2 * N * WIDE, transcendentals=0),
    )(place, sizes, pattern, aux)


def tiles(p):
    for t in range(N // TILE):
        other, within = divmod(t * TILE, HALF)
        swapped = (1 - other) * HALF + within
        at = other * (WIDE // 2) + p * HALF + within
        yield slice(t * TILE, (t + 1) * TILE), slice(swapped, swapped + TILE), slice(at, at + TILE)


def first_kernel(send_own, mine, part):
    for p in range(P_DEV):
        for s, _, at in tiles(p):
            part[:, at] = lax.dot_general(send_own[p], mine[:, s], NN, preferred_element_type=F32)


def first_part(send_own, mine):
    return pl.pallas_call(
        first_kernel,
        in_specs=[VMEM, VMEM],
        out_specs=VMEM,
        out_shape=jax.ShapeDtypeStruct((HALF, WIDE), F32),
        compiler_params=params(20),
        cost_estimate=cost(0.5),
    )(send_own, mine)


def part_sums(aux, coeff, store):
    rows = jnp.concatenate(
        [
            jnp.concatenate([quarter[p] for quarter in half for p in range(P_DEV)], axis=1)
            for half in (aux[:2], aux[2:])
        ],
        axis=0,
    )
    value = lax.dot_general(rows, coeff[...], NT, preferred_element_type=F32)
    for h in range(TILE // BS):
        store(h, value[:, h * BS:(h + 1) * BS])


def part_rows(far):
    return slice(TILE, 2 * TILE) if far else slice(0, TILE)


def send_kernel(far, send_own, send_other, keep_own, keep_other, theirs, part, out, coeff):
    rows = part_rows(far)
    for p in range(P_DEV):
        for s, swapped, at in tiles(p):
            value = lax.dot_general(send_other[p, rows], theirs[:, swapped], NN, preferred_element_type=F32)
            coeff[:, at] = (part[rows, at] + value).astype(BF16)

    def store(h, value):
        out[h] = value

    part_sums((send_own, send_other, keep_own, keep_other), coeff, store)


def send_sums(far, aux, theirs, part):
    return pl.pallas_call(
        functools.partial(send_kernel, far),
        in_specs=[VMEM] * 6,
        out_specs=VMEM,
        out_shape=jax.ShapeDtypeStruct((TILE // BS, N, BS), F32),
        scratch_shapes=[pltpu.VMEM((TILE, WIDE), BF16)],
        compiler_params=params(20),
        cost_estimate=cost(0.75),
    )(*aux, theirs, part)


def keep_coeff(far, keep_own, keep_other, mine, theirs, coeff):
    for p in range(P_DEV):
        rows = jnp.concatenate([keep_own[p, part_rows(far)], keep_other[p, part_rows(far)]], axis=1)
        for s, swapped, at in tiles(p):
            dens = jnp.concatenate([mine[:, s], theirs[:, swapped]], axis=0)
            coeff[:, at] = lax.dot_general(rows, dens, NN, preferred_element_type=F32).astype(BF16)


def other_order(got, h):
    return jnp.concatenate([got[h, HALF:, :], got[h, :HALF, :]], axis=0)


def near_kernel(place, send_own, send_other, keep_own, keep_other, mine, theirs, got, up, down, coeff):
    keep_coeff(False, keep_own, keep_other, mine, theirs, coeff)
    first_up = (place[2] == 0) | (place[2] == 3)

    def store(h, value):
        value = (value + other_order(got, h)).astype(BF16)
        goes_up = first_up if h == 0 else jnp.logical_not(first_up)

        @pl.when(goes_up)
        def _():
            up[...] = value

        @pl.when(jnp.logical_not(goes_up))
        def _():
            down[...] = value

    part_sums((send_own, send_other, keep_own, keep_other), coeff, store)


def near_sums(place, aux, mine, theirs, got):
    return pl.pallas_call(
        near_kernel,
        in_specs=[SMEM] + [VMEM] * 7,
        out_specs=[VMEM, VMEM],
        out_shape=[jax.ShapeDtypeStruct((N, BS), BF16)] * 2,
        scratch_shapes=[pltpu.VMEM((TILE, WIDE), BF16)],
        compiler_params=params(20),
        cost_estimate=cost(1),
    )(place, *aux, mine, theirs, got)


def far_kernel(send_own, send_other, keep_own, keep_other, mine, theirs, got, out, coeff):
    keep_coeff(True, keep_own, keep_other, mine, theirs, coeff)

    def store(h, value):
        out[h] = value + other_order(got, h)

    part_sums((send_own, send_other, keep_own, keep_other), coeff, store)


def far_sums(aux, mine, theirs, got):
    return pl.pallas_call(
        far_kernel,
        in_specs=[VMEM] * 7,
        out_specs=VMEM,
        out_shape=jax.ShapeDtypeStruct((TILE // BS, N, BS), F32),
        scratch_shapes=[pltpu.VMEM((TILE, WIDE), BF16)],
        compiler_params=params(20),
        cost_estimate=cost(1),
    )(*aux, mine, theirs, got)


def join_kernel(place, far, low, high, out):
    for i, j in enumerate((1, 0, 3, 2)):
        to, at = slice(i * TILE, (i + 1) * TILE), slice(j * TILE, (j + 1) * TILE)
        both = low[at, :].astype(F32) + high[at, :].astype(F32)
        for h in range(TILE // BS):
            own = (place[2] // 2 == h).astype(F32)
            out[h, to, :] = (far[h, to, :] + both * own).astype(BF16)


def join(place, far, low, high):
    return pl.pallas_call(
        join_kernel,
        in_specs=[SMEM, VMEM, VMEM, VMEM],
        out_specs=VMEM,
        out_shape=jax.ShapeDtypeStruct((TILE // BS, N, BS), BF16),
        compiler_params=params(20),
    )(place, far, low, high)


def finish_kernel(parts, out):
    out[...] = jnp.sum(parts[...].astype(F32), axis=0)


def finish(parts):
    return pl.pallas_call(
        finish_kernel,
        in_specs=[VMEM],
        out_specs=VMEM,
        out_shape=jax.ShapeDtypeStruct((BS // 2, BS), F32),
        compiler_params=params(16),
    )(parts)


def sums_groups():
    def second(core, odd):
        order = row_order(core, odd)
        return order[NB // 2:] + order[:NB // 2]

    return [
        [(z * 2 + core) * 16 + 2 * b + h for z in (odd, odd + 2) for b in second(core, odd) for h in range(2)]
        for odd in range(2)
        for core in range(2)
    ]


def local(aux_ints, density, pattern, block_sizes):
    core = lax.axis_index("c")
    z = lax.axis_index("z")
    place = jnp.stack([core, lax.rem(z, 2), z])

    def swap(array):
        return lax.ppermute(array, "c", [(0, 1), (1, 0)])

    blocks = density.reshape(ROWS, NB // 2, 2, BS).swapaxes(1, 2)
    blocks = jnp.where(core == 0, blocks, blocks[:, ::-1]).reshape(ROWS, N)
    everyone = jnp.broadcast_to(blocks[None], (CHIP_COUNT, ROWS, N))
    mine = lax.all_to_all(everyone, CHIPS, 0, 0).reshape(HALF, N)
    mine, aux = lax.optimization_barrier((mine, prepare(place, block_sizes, pattern, aux_ints)))
    theirs = swap(mine)
    part = first_part(aux[0], mine)
    got = swap(send_sums(False, aux, theirs, part))
    up, down = near_sums(place, aux, mine, theirs, got)
    low = lax.ppermute(up, "z", [(i, (i + 1) % 4) for i in range(4)])
    high = lax.ppermute(down, "z", [(i, (i - 1) % 4) for i in range(4)])
    got = swap(send_sums(True, aux, theirs, part))
    far = far_sums(aux, mine, theirs, got)
    chip = join(place, far, low, high)
    chip = chip.reshape(CHIP_COUNT // 2, BS // 2, BS)
    parts = lax.all_to_all(chip, ("z", "c", "x", "y"), 0, 0, axis_index_groups=sums_groups())
    return finish(parts).T


def solution(mesh):
    whole = Mesh(mesh.devices.reshape(4, 2, 4, 4), ("z", "c", "x", "y"))
    everywhere = ("z", "c", "x", "y")
    in_specs = (P(everywhere, None, None), P(everywhere, None), P(everywhere, None, None), P())
    return jax.shard_map(local, mesh=whole, in_specs=in_specs, out_specs=P(("z", "c"), ("x", "y")), check_vma=False)
```

```python
import functools

import jax
import jax.numpy as jnp
from jax import lax
from jax.experimental import pallas as pl
from jax.experimental.pallas import tpu as pltpu
from jax.sharding import Mesh, PartitionSpec as P

F32 = jnp.float32
BF16 = jnp.bfloat16
BS = 128
NB = 8
N = BS * NB
P_DEV = 4
WIDE = P_DEV * N
HALF = N // 2
TILE = 256
CHIP_COUNT = 64
ROWS = 8
NN = (((1,), (0,)), ((), ()))
NT = (((1,), (1,)), ((), ()))
CHIPS = ("z", "x", "y")
SMEM = pl.BlockSpec(memory_space=pltpu.SMEM)
VMEM = pl.BlockSpec(memory_space=pltpu.VMEM)


def params(mib):
    return pltpu.CompilerParams(vmem_limit_bytes=mib * 2**20)


def cost(products):
    return pl.CostEstimate(flops=int(products * N * N * WIDE), bytes_accessed=0, transcendentals=0)


def core_order(core):
    return [2 * z + core for z in range(NB // 2)] + [2 * z + 1 - core for z in range(NB // 2)]


def row_order(core, odd):
    zs = (1 - odd, 3 - odd, odd, odd + 2)
    return [2 * z + core for z in zs] + [2 * z + 1 - core for z in zs]


def block(index):
    return pl.ds(pl.multiple_of(index * BS, BS), BS)


def prepare_kernel(place, sizes, pattern, aux, send_own, send_other, keep_own, keep_other):
    p = pl.program_id(0)
    lane = lax.broadcasted_iota(jnp.int32, (1, BS), 1)
    row = lax.broadcasted_iota(jnp.int32, (BS, 1), 0)
    order = core_order(place[0])
    rows_order = row_order(place[0], place[1])
    cols = [((lane < sizes[b]) & (pattern[p, b, b] > 0)).astype(F32) for b in order]
    outs = ((keep_own, keep_other), (send_own, send_other))
    for i, b in enumerate(rows_order):
        rows = ((row < sizes[b]) & (pattern[p, b, b] > 0)).astype(F32)
        half, at = divmod(i, NB // 2)
        for j, k in enumerate(order):
            value = aux[0, block(b), block(k)] * (rows * cols[j]).astype(BF16)
            other, to = divmod(j, NB // 2)
            which = p if half and not other else 0
            outs[half][other][which, at * BS:(at + 1) * BS, to * BS:(to + 1) * BS] = value


def prepare(place, sizes, pattern, aux):
    quarter = pl.BlockSpec((1, HALF, HALF), lambda p: (p, 0, 0))
    return pl.pallas_call(
        prepare_kernel,
        grid=(P_DEV,),
        in_specs=[SMEM, SMEM, SMEM, pl.BlockSpec((1, N, N), lambda p: (p, 0, 0))],
        out_specs=[VMEM] + [quarter] * 3,
        out_shape=[jax.ShapeDtypeStruct((P_DEV, HALF, HALF), BF16)] + [pltpu.HBM((P_DEV, HALF, HALF), BF16)] * 3,
        compiler_params=params(48),
        cost_estimate=pl.CostEstimate(flops=0, bytes_accessed=2 * 2 * N * WIDE, transcendentals=0),
    )(place, sizes, pattern, aux)


def tiles(p):
    for t in range(N // TILE):
        other, within = divmod(t * TILE, HALF)
        swapped = (1 - other) * HALF + within
        at = other * (WIDE // 2) + p * HALF + within
        yield slice(t * TILE, (t + 1) * TILE), slice(swapped, swapped + TILE), slice(at, at + TILE)


def first_kernel(send_own, mine, part):
    for p in range(P_DEV):
        for s, _, at in tiles(p):
            part[:, at] = lax.dot_general(send_own[p], mine[:, s], NN, preferred_element_type=F32)


def first_part(send_own, mine):
    return pl.pallas_call(
        first_kernel,
        in_specs=[VMEM, VMEM],
        out_specs=VMEM,
        out_shape=jax.ShapeDtypeStruct((HALF, WIDE), F32),
        compiler_params=params(20),
        cost_estimate=cost(0.5),
    )(send_own, mine)


def part_sums(aux, coeff, store):
    rows = jnp.concatenate(
        [
            jnp.concatenate([quarter[p] for quarter in half for p in range(P_DEV)], axis=1)
            for half in (aux[:2], aux[2:])
        ],
        axis=0,
    )
    value = lax.dot_general(rows, coeff[...], NT, preferred_element_type=F32)
    for h in range(TILE // BS):
        store(h, value[:, h * BS:(h + 1) * BS])


def part_rows(far):
    return slice(TILE, 2 * TILE) if far else slice(0, TILE)


def send_kernel(far, send_own, send_other, keep_own, keep_other, theirs, part, out, coeff):
    rows = part_rows(far)
    for p in range(P_DEV):
        for s, swapped, at in tiles(p):
            value = lax.dot_general(send_other[p, rows], theirs[:, swapped], NN, preferred_element_type=F32)
            coeff[:, at] = (part[rows, at] + value).astype(BF16)

    def store(h, value):
        out[h] = value

    part_sums((send_own, send_other, keep_own, keep_other), coeff, store)


def send_sums(far, aux, theirs, part):
    return pl.pallas_call(
        functools.partial(send_kernel, far),
        in_specs=[VMEM] * 6,
        out_specs=VMEM,
        out_shape=jax.ShapeDtypeStruct((TILE // BS, N, BS), F32),
        scratch_shapes=[pltpu.VMEM((TILE, WIDE), BF16)],
        compiler_params=params(20),
        cost_estimate=cost(0.75),
    )(*aux, theirs, part)


def keep_coeff(far, keep_own, keep_other, mine, theirs, coeff):
    for p in range(P_DEV):
        rows = jnp.concatenate([keep_own[p, part_rows(far)], keep_other[p, part_rows(far)]], axis=1)
        for s, swapped, at in tiles(p):
            dens = jnp.concatenate([mine[:, s], theirs[:, swapped]], axis=0)
            coeff[:, at] = lax.dot_general(rows, dens, NN, preferred_element_type=F32).astype(BF16)


def other_order(got, h):
    return jnp.concatenate([got[h, HALF:, :], got[h, :HALF, :]], axis=0)


def near_kernel(send_own, send_other, keep_own, keep_other, mine, theirs, got, up, down, coeff):
    keep_coeff(False, keep_own, keep_other, mine, theirs, coeff)
    z = lax.axis_index("z")
    first_up = (z == 0) | (z == 3)

    def store(h, value):
        value = (value + other_order(got, h)).astype(BF16)
        goes_up = first_up if h == 0 else jnp.logical_not(first_up)

        @pl.when(goes_up)
        def _():
            up[...] = value

        @pl.when(jnp.logical_not(goes_up))
        def _():
            down[...] = value

    part_sums((send_own, send_other, keep_own, keep_other), coeff, store)


def near_sums(aux, mine, theirs, got):
    return pl.pallas_call(
        near_kernel,
        in_specs=[VMEM] * 7,
        out_specs=[VMEM, VMEM],
        out_shape=[jax.ShapeDtypeStruct((N, BS), BF16)] * 2,
        scratch_shapes=[pltpu.VMEM((TILE, WIDE), BF16)],
        compiler_params=params(20),
        cost_estimate=cost(1),
    )(*aux, mine, theirs, got)


def far_kernel(send_own, send_other, keep_own, keep_other, mine, theirs, got, out, coeff):
    keep_coeff(True, keep_own, keep_other, mine, theirs, coeff)

    def store(h, value):
        out[h] = value + other_order(got, h)

    part_sums((send_own, send_other, keep_own, keep_other), coeff, store)


def far_sums(aux, mine, theirs, got):
    return pl.pallas_call(
        far_kernel,
        in_specs=[VMEM] * 7,
        out_specs=VMEM,
        out_shape=jax.ShapeDtypeStruct((TILE // BS, N, BS), F32),
        scratch_shapes=[pltpu.VMEM((TILE, WIDE), BF16)],
        compiler_params=params(20),
        cost_estimate=cost(1),
    )(*aux, mine, theirs, got)


def join_kernel(far, low, high, out):
    own_slot = lax.axis_index("z") // 2
    for i, j in enumerate((1, 0, 3, 2)):
        to, at = slice(i * TILE, (i + 1) * TILE), slice(j * TILE, (j + 1) * TILE)
        both = low[at, :].astype(F32) + high[at, :].astype(F32)
        for h in range(TILE // BS):
            own = (own_slot == h).astype(F32)
            out[h, to, :] = (far[h, to, :] + both * own).astype(BF16)


def join(far, low, high):
    return pl.pallas_call(
        join_kernel,
        in_specs=[VMEM, VMEM, VMEM],
        out_specs=VMEM,
        out_shape=jax.ShapeDtypeStruct((TILE // BS, N, BS), BF16),
        compiler_params=params(20),
    )(far, low, high)


def finish_kernel(parts, out):
    out[...] = jnp.sum(parts[...].astype(F32), axis=0)


def finish(parts):
    return pl.pallas_call(
        finish_kernel,
        in_specs=[VMEM],
        out_specs=VMEM,
        out_shape=jax.ShapeDtypeStruct((BS // 2, BS), F32),
        compiler_params=params(16),
    )(parts)


def sums_groups():
    def second(core, odd):
        order = row_order(core, odd)
        return order[NB // 2:] + order[:NB // 2]

    return [
        [(z * 2 + core) * 16 + 2 * b + h for z in (odd, odd + 2) for b in second(core, odd) for h in range(2)]
        for odd in range(2)
        for core in range(2)
    ]


def local(aux_ints, density, pattern, block_sizes):
    core = lax.axis_index("c")
    place = jnp.stack([core, lax.rem(lax.axis_index("z"), 2)])

    def swap(array):
        return lax.ppermute(array, "c", [(0, 1), (1, 0)])

    blocks = density.reshape(ROWS, NB // 2, 2, BS).swapaxes(1, 2)
    blocks = jnp.where(core == 0, blocks, blocks[:, ::-1]).reshape(ROWS, N)
    everyone = jnp.broadcast_to(blocks[None], (CHIP_COUNT, ROWS, N))
    mine = lax.all_to_all(everyone, CHIPS, 0, 0).reshape(HALF, N)
    mine, aux = lax.optimization_barrier((mine, prepare(place, block_sizes, pattern, aux_ints)))
    theirs = swap(mine)
    part = first_part(aux[0], mine)
    got = swap(send_sums(False, aux, theirs, part))
    up, down = near_sums(aux, mine, theirs, got)
    low = lax.ppermute(up, "z", [(i, (i + 1) % 4) for i in range(4)])
    high = lax.ppermute(down, "z", [(i, (i - 1) % 4) for i in range(4)])
    got = swap(send_sums(True, aux, theirs, part))
    far = far_sums(aux, mine, theirs, got)
    chip = join(far, low, high)
    chip = chip.reshape(CHIP_COUNT // 2, BS // 2, BS)
    parts = lax.all_to_all(chip, ("z", "c", "x", "y"), 0, 0, axis_index_groups=sums_groups())
    return finish(parts).T


def solution(mesh):
    whole = Mesh(mesh.devices.reshape(4, 2, 4, 4), ("z", "c", "x", "y"))
    everywhere = ("z", "c", "x", "y")
    in_specs = (P(everywhere, None, None), P(everywhere, None), P(everywhere, None, None), P())
    return jax.shard_map(local, mesh=whole, in_specs=in_specs, out_specs=P(("z", "c"), ("x", "y")), check_vma=False)
```

```python
import functools

import jax
import jax.numpy as jnp
from jax import lax
from jax.experimental import pallas as pl
from jax.experimental.pallas import tpu as pltpu
from jax.sharding import Mesh, PartitionSpec as P

F32 = jnp.float32
BF16 = jnp.bfloat16
BS = 128
NB = 8
N = BS * NB
P_DEV = 4
WIDE = P_DEV * N
HALF = N // 2
TILE = 256
CHIP_COUNT = 64
ROWS = 8
SPREAD = 8
NN = (((1,), (0,)), ((), ()))
NT = (((1,), (1,)), ((), ()))
CHIPS = ("z", "x", "y")
SMEM = pl.BlockSpec(memory_space=pltpu.SMEM)
VMEM = pl.BlockSpec(memory_space=pltpu.VMEM)


def params(mib):
    return pltpu.CompilerParams(vmem_limit_bytes=mib * 2**20)


def cost(products):
    return pl.CostEstimate(flops=int(products * N * N * WIDE), bytes_accessed=0, transcendentals=0)


def core_order(core):
    return [2 * z + core for z in range(NB // 2)] + [2 * z + 1 - core for z in range(NB // 2)]


def row_order(core, odd):
    zs = (1 - odd, 3 - odd, odd, odd + 2)
    return [2 * z + core for z in zs] + [2 * z + 1 - core for z in zs]


def block(index):
    return pl.ds(pl.multiple_of(index * BS, BS), BS)


def spread_kernel(dens, out, copies, sems):
    order = core_order(lax.axis_index("c"))
    rows = jnp.concatenate([dens[:, block(b)] for b in order], axis=1)
    for i in range(SPREAD):
        copies[i] = rows
    sends = [pltpu.make_async_copy(copies, out.at[i * SPREAD:(i + 1) * SPREAD], sems.at[i]) for i in range(CHIP_COUNT // SPREAD)]
    for send in sends:
        send.start()
    for send in sends:
        send.wait()


def spread(density):
    return pl.pallas_call(
        spread_kernel,
        in_specs=[VMEM],
        out_specs=pl.BlockSpec(memory_space=pltpu.HBM),
        out_shape=pltpu.HBM((CHIP_COUNT, ROWS, N), BF16),
        scratch_shapes=[pltpu.VMEM((SPREAD, ROWS, N), BF16), pltpu.SemaphoreType.DMA((CHIP_COUNT // SPREAD,))],
        compiler_params=params(8),
    )(density)


def prepare_kernel(place, sizes, pattern, aux, send_own, send_other, keep_own, keep_other):
    p = pl.program_id(0)
    lane = lax.broadcasted_iota(jnp.int32, (1, BS), 1)
    row = lax.broadcasted_iota(jnp.int32, (BS, 1), 0)
    order = core_order(place[0])
    rows_order = row_order(place[0], place[1])
    cols = [((lane < sizes[b]) & (pattern[p, b, b] > 0)).astype(F32) for b in order]
    outs = ((keep_own, keep_other), (send_own, send_other))
    for i, b in enumerate(rows_order):
        rows = ((row < sizes[b]) & (pattern[p, b, b] > 0)).astype(F32)
        half, at = divmod(i, NB // 2)
        for j, k in enumerate(order):
            value = aux[0, block(b), block(k)] * (rows * cols[j]).astype(BF16)
            other, to = divmod(j, NB // 2)
            which = p if half and not other else 0
            outs[half][other][which, at * BS:(at + 1) * BS, to * BS:(to + 1) * BS] = value


def prepare(place, sizes, pattern, aux):
    quarter = pl.BlockSpec((1, HALF, HALF), lambda p: (p, 0, 0))
    return pl.pallas_call(
        prepare_kernel,
        grid=(P_DEV,),
        in_specs=[SMEM, SMEM, SMEM, pl.BlockSpec((1, N, N), lambda p: (p, 0, 0))],
        out_specs=[VMEM] + [quarter] * 3,
        out_shape=[jax.ShapeDtypeStruct((P_DEV, HALF, HALF), BF16)] + [pltpu.HBM((P_DEV, HALF, HALF), BF16)] * 3,
        compiler_params=params(48),
        cost_estimate=pl.CostEstimate(flops=0, bytes_accessed=2 * 2 * N * WIDE, transcendentals=0),
    )(place, sizes, pattern, aux)


def tiles(p):
    for t in range(N // TILE):
        other, within = divmod(t * TILE, HALF)
        swapped = (1 - other) * HALF + within
        at = other * (WIDE // 2) + p * HALF + within
        yield slice(t * TILE, (t + 1) * TILE), slice(swapped, swapped + TILE), slice(at, at + TILE)


def first_kernel(send_own, mine, part):
    for p in range(P_DEV):
        for s, _, at in tiles(p):
            part[:, at] = lax.dot_general(send_own[p], mine[:, s], NN, preferred_element_type=F32)


def first_part(send_own, mine):
    return pl.pallas_call(
        first_kernel,
        in_specs=[VMEM, VMEM],
        out_specs=VMEM,
        out_shape=jax.ShapeDtypeStruct((HALF, WIDE), F32),
        compiler_params=params(20),
        cost_estimate=cost(0.5),
    )(send_own, mine)


def part_sums(aux, coeff, store):
    rows = jnp.concatenate(
        [
            jnp.concatenate([quarter[p] for quarter in half for p in range(P_DEV)], axis=1)
            for half in (aux[:2], aux[2:])
        ],
        axis=0,
    )
    value = lax.dot_general(rows, coeff[...], NT, preferred_element_type=F32)
    for h in range(TILE // BS):
        store(h, value[:, h * BS:(h + 1) * BS])


def part_rows(far):
    return slice(TILE, 2 * TILE) if far else slice(0, TILE)


def send_kernel(far, send_own, send_other, keep_own, keep_other, theirs, part, out, coeff):
    rows = part_rows(far)
    for p in range(P_DEV):
        for s, swapped, at in tiles(p):
            value = lax.dot_general(send_other[p, rows], theirs[:, swapped], NN, preferred_element_type=F32)
            coeff[:, at] = (part[rows, at] + value).astype(BF16)

    def store(h, value):
        out[h] = value

    part_sums((send_own, send_other, keep_own, keep_other), coeff, store)


def send_sums(far, aux, theirs, part):
    return pl.pallas_call(
        functools.partial(send_kernel, far),
        in_specs=[VMEM] * 6,
        out_specs=VMEM,
        out_shape=jax.ShapeDtypeStruct((TILE // BS, N, BS), F32),
        scratch_shapes=[pltpu.VMEM((TILE, WIDE), BF16)],
        compiler_params=params(20),
        cost_estimate=cost(0.75),
    )(*aux, theirs, part)


def keep_coeff(far, keep_own, keep_other, mine, theirs, coeff):
    for p in range(P_DEV):
        rows = jnp.concatenate([keep_own[p, part_rows(far)], keep_other[p, part_rows(far)]], axis=1)
        for s, swapped, at in tiles(p):
            dens = jnp.concatenate([mine[:, s], theirs[:, swapped]], axis=0)
            coeff[:, at] = lax.dot_general(rows, dens, NN, preferred_element_type=F32).astype(BF16)


def other_order(got, h):
    return jnp.concatenate([got[h, HALF:, :], got[h, :HALF, :]], axis=0)


def near_kernel(send_own, send_other, keep_own, keep_other, mine, theirs, got, up, down, coeff):
    keep_coeff(False, keep_own, keep_other, mine, theirs, coeff)
    z = lax.axis_index("z")
    first_up = (z == 0) | (z == 3)

    def store(h, value):
        value = (value + other_order(got, h)).astype(BF16)
        goes_up = first_up if h == 0 else jnp.logical_not(first_up)

        @pl.when(goes_up)
        def _():
            up[...] = value

        @pl.when(jnp.logical_not(goes_up))
        def _():
            down[...] = value

    part_sums((send_own, send_other, keep_own, keep_other), coeff, store)


def near_sums(aux, mine, theirs, got):
    return pl.pallas_call(
        near_kernel,
        in_specs=[VMEM] * 7,
        out_specs=[VMEM, VMEM],
        out_shape=[jax.ShapeDtypeStruct((N, BS), BF16)] * 2,
        scratch_shapes=[pltpu.VMEM((TILE, WIDE), BF16)],
        compiler_params=params(20),
        cost_estimate=cost(1),
    )(*aux, mine, theirs, got)


def far_kernel(send_own, send_other, keep_own, keep_other, mine, theirs, got, out, coeff):
    keep_coeff(True, keep_own, keep_other, mine, theirs, coeff)

    def store(h, value):
        out[h] = value + other_order(got, h)

    part_sums((send_own, send_other, keep_own, keep_other), coeff, store)


def far_sums(aux, mine, theirs, got):
    return pl.pallas_call(
        far_kernel,
        in_specs=[VMEM] * 7,
        out_specs=VMEM,
        out_shape=jax.ShapeDtypeStruct((TILE // BS, N, BS), F32),
        scratch_shapes=[pltpu.VMEM((TILE, WIDE), BF16)],
        compiler_params=params(20),
        cost_estimate=cost(1),
    )(*aux, mine, theirs, got)


def join_kernel(far, low, high, out):
    own_slot = lax.axis_index("z") // 2
    for i, j in enumerate((1, 0, 3, 2)):
        to, at = slice(i * TILE, (i + 1) * TILE), slice(j * TILE, (j + 1) * TILE)
        both = low[at, :].astype(F32) + high[at, :].astype(F32)
        for h in range(TILE // BS):
            own = (own_slot == h).astype(F32)
            out[h, to, :] = (far[h, to, :] + both * own).astype(BF16)


def join(far, low, high):
    return pl.pallas_call(
        join_kernel,
        in_specs=[VMEM, VMEM, VMEM],
        out_specs=VMEM,
        out_shape=jax.ShapeDtypeStruct((TILE // BS, N, BS), BF16),
        compiler_params=params(20),
    )(far, low, high)


def finish_kernel(parts, out):
    out[...] = jnp.sum(parts[...].astype(F32), axis=0)


def finish(parts):
    return pl.pallas_call(
        finish_kernel,
        in_specs=[VMEM],
        out_specs=VMEM,
        out_shape=jax.ShapeDtypeStruct((BS // 2, BS), F32),
        compiler_params=params(16),
    )(parts)


def sums_groups():
    def second(core, odd):
        order = row_order(core, odd)
        return order[NB // 2:] + order[:NB // 2]

    return [
        [(z * 2 + core) * 16 + 2 * b + h for z in (odd, odd + 2) for b in second(core, odd) for h in range(2)]
        for odd in range(2)
        for core in range(2)
    ]


def local(aux_ints, density, pattern, block_sizes):
    core = lax.axis_index("c")
    place = jnp.stack([core, lax.rem(lax.axis_index("z"), 2)])

    def swap(array):
        return lax.ppermute(array, "c", [(0, 1), (1, 0)])

    mine = lax.all_to_all(spread(density), CHIPS, 0, 0).reshape(HALF, N)
    mine, aux = lax.optimization_barrier((mine, prepare(place, block_sizes, pattern, aux_ints)))
    theirs = swap(mine)
    part = first_part(aux[0], mine)
    got = swap(send_sums(False, aux, theirs, part))
    up, down = near_sums(aux, mine, theirs, got)
    low = lax.ppermute(up, "z", [(i, (i + 1) % 4) for i in range(4)])
    high = lax.ppermute(down, "z", [(i, (i - 1) % 4) for i in range(4)])
    got = swap(send_sums(True, aux, theirs, part))
    far = far_sums(aux, mine, theirs, got)
    chip = join(far, low, high)
    chip = chip.reshape(CHIP_COUNT // 2, BS // 2, BS)
    parts = lax.all_to_all(chip, ("z", "c", "x", "y"), 0, 0, axis_index_groups=sums_groups())
    return finish(parts).T


def solution(mesh):
    whole = Mesh(mesh.devices.reshape(4, 2, 4, 4), ("z", "c", "x", "y"))
    everywhere = ("z", "c", "x", "y")
    in_specs = (P(everywhere, None, None), P(everywhere, None), P(everywhere, None, None), P())
    return jax.shard_map(local, mesh=whole, in_specs=in_specs, out_specs=P(("z", "c"), ("x", "y")), check_vma=False)
```

```python
import functools

import jax
import jax.numpy as jnp
from jax import lax
from jax.experimental import pallas as pl
from jax.experimental.pallas import tpu as pltpu
from jax.sharding import Mesh, PartitionSpec as P

F32 = jnp.float32
BF16 = jnp.bfloat16
BS = 128
NB = 8
N = BS * NB
P_DEV = 4
WIDE = P_DEV * N
HALF = N // 2
TILE = 256
CHIP_COUNT = 64
ROWS = 8
NN = (((1,), (0,)), ((), ()))
NT = (((1,), (1,)), ((), ()))
CHIPS = ("z", "x", "y")
SMEM = pl.BlockSpec(memory_space=pltpu.SMEM)
VMEM = pl.BlockSpec(memory_space=pltpu.VMEM)


def params(mib):
    return pltpu.CompilerParams(vmem_limit_bytes=mib * 2**20)


def cost(products):
    return pl.CostEstimate(flops=int(products * N * N * WIDE), bytes_accessed=0, transcendentals=0)


def core_order(core):
    return [2 * z + core for z in range(NB // 2)] + [2 * z + 1 - core for z in range(NB // 2)]


def row_order(core, odd):
    zs = (1 - odd, 3 - odd, odd, odd + 2)
    return [2 * z + core for z in zs] + [2 * z + 1 - core for z in zs]


def block(index):
    return pl.ds(pl.multiple_of(index * BS, BS), BS)


def prepare_kernel(place, sizes, pattern, aux, send_own, send_other, keep_own, keep_other):
    p = pl.program_id(0)
    lane = lax.broadcasted_iota(jnp.int32, (1, BS), 1)
    row = lax.broadcasted_iota(jnp.int32, (BS, 1), 0)
    order = core_order(place[0])
    rows_order = row_order(place[0], place[1])
    cols = [((lane < sizes[b]) & (pattern[p, b, b] > 0)).astype(F32) for b in order]
    outs = ((keep_own, keep_other), (send_own, send_other))
    for i, b in enumerate(rows_order):
        rows = ((row < sizes[b]) & (pattern[p, b, b] > 0)).astype(F32)
        half, at = divmod(i, NB // 2)
        for j, k in enumerate(order):
            value = aux[0, block(b), block(k)] * (rows * cols[j]).astype(BF16)
            other, to = divmod(j, NB // 2)
            which = p if half and not other else 0
            outs[half][other][which, at * BS:(at + 1) * BS, to * BS:(to + 1) * BS] = value


def prepare(place, sizes, pattern, aux):
    quarter = pl.BlockSpec((1, HALF, HALF), lambda p: (p, 0, 0))
    return pl.pallas_call(
        prepare_kernel,
        grid=(P_DEV,),
        in_specs=[SMEM, SMEM, SMEM, pl.BlockSpec((1, N, N), lambda p: (p, 0, 0))],
        out_specs=[VMEM] + [quarter] * 3,
        out_shape=[jax.ShapeDtypeStruct((P_DEV, HALF, HALF), BF16)] + [pltpu.HBM((P_DEV, HALF, HALF), BF16)] * 3,
        compiler_params=params(48),
        cost_estimate=pl.CostEstimate(flops=0, bytes_accessed=2 * 2 * N * WIDE, transcendentals=0),
    )(place, sizes, pattern, aux)


def tiles(p):
    for t in range(N // TILE):
        other, within = divmod(t * TILE, HALF)
        swapped = (1 - other) * HALF + within
        at = other * (WIDE // 2) + p * HALF + within
        yield slice(t * TILE, (t + 1) * TILE), slice(swapped, swapped + TILE), slice(at, at + TILE)


def first_kernel(send_own, mine, part):
    for p in range(P_DEV):
        for s, _, at in tiles(p):
            part[:, at] = lax.dot_general(send_own[p], mine[:, s], NN, preferred_element_type=F32)


def first_part(send_own, mine):
    return pl.pallas_call(
        first_kernel,
        in_specs=[VMEM, VMEM],
        out_specs=VMEM,
        out_shape=jax.ShapeDtypeStruct((HALF, WIDE), F32),
        compiler_params=params(20),
        cost_estimate=cost(0.5),
    )(send_own, mine)


def part_sums(aux, coeff, store):
    rows = jnp.concatenate(
        [
            jnp.concatenate([quarter[p] for quarter in half for p in range(P_DEV)], axis=1)
            for half in (aux[:2], aux[2:])
        ],
        axis=0,
    )
    value = lax.dot_general(rows, coeff[...], NT, preferred_element_type=F32)
    for h in range(TILE // BS):
        store(h, value[:, h * BS:(h + 1) * BS])


def part_rows(far):
    return slice(TILE, 2 * TILE) if far else slice(0, TILE)


def send_kernel(far, send_own, send_other, keep_own, keep_other, theirs, part, out, coeff):
    rows = part_rows(far)
    for p in range(P_DEV):
        for s, swapped, at in tiles(p):
            value = lax.dot_general(send_other[p, rows], theirs[:, swapped], NN, preferred_element_type=F32)
            coeff[:, at] = (part[rows, at] + value).astype(BF16)

    def store(h, value):
        out[h] = value

    part_sums((send_own, send_other, keep_own, keep_other), coeff, store)


def send_sums(far, aux, theirs, part):
    return pl.pallas_call(
        functools.partial(send_kernel, far),
        in_specs=[VMEM] * 6,
        out_specs=VMEM,
        out_shape=jax.ShapeDtypeStruct((TILE // BS, N, BS), F32),
        scratch_shapes=[pltpu.VMEM((TILE, WIDE), BF16)],
        compiler_params=params(20),
        cost_estimate=cost(0.75),
    )(*aux, theirs, part)


def keep_coeff(far, keep_own, keep_other, mine, theirs, coeff):
    for p in range(P_DEV):
        rows = jnp.concatenate([keep_own[p, part_rows(far)], keep_other[p, part_rows(far)]], axis=1)
        for s, swapped, at in tiles(p):
            dens = jnp.concatenate([mine[:, s], theirs[:, swapped]], axis=0)
            coeff[:, at] = lax.dot_general(rows, dens, NN, preferred_element_type=F32).astype(BF16)


def other_order(got, h):
    return jnp.concatenate([got[h, HALF:, :], got[h, :HALF, :]], axis=0)


def near_kernel(send_own, send_other, keep_own, keep_other, mine, theirs, got, up, down, coeff):
    keep_coeff(False, keep_own, keep_other, mine, theirs, coeff)
    z = lax.axis_index("z")
    first_up = (z == 0) | (z == 3)

    def store(h, value):
        value = (value + other_order(got, h)).astype(BF16)
        goes_up = first_up if h == 0 else jnp.logical_not(first_up)

        @pl.when(goes_up)
        def _():
            up[...] = value

        @pl.when(jnp.logical_not(goes_up))
        def _():
            down[...] = value

    part_sums((send_own, send_other, keep_own, keep_other), coeff, store)


def near_sums(aux, mine, theirs, got):
    return pl.pallas_call(
        near_kernel,
        in_specs=[VMEM] * 7,
        out_specs=[VMEM, VMEM],
        out_shape=[jax.ShapeDtypeStruct((N, BS), BF16)] * 2,
        scratch_shapes=[pltpu.VMEM((TILE, WIDE), BF16)],
        compiler_params=params(20),
        cost_estimate=cost(1),
    )(*aux, mine, theirs, got)


def far_kernel(send_own, send_other, keep_own, keep_other, mine, theirs, got, out, coeff):
    keep_coeff(True, keep_own, keep_other, mine, theirs, coeff)

    def store(h, value):
        out[h] = value + other_order(got, h)

    part_sums((send_own, send_other, keep_own, keep_other), coeff, store)


def far_sums(aux, mine, theirs, got):
    return pl.pallas_call(
        far_kernel,
        in_specs=[VMEM] * 7,
        out_specs=VMEM,
        out_shape=jax.ShapeDtypeStruct((TILE // BS, N, BS), F32),
        scratch_shapes=[pltpu.VMEM((TILE, WIDE), BF16)],
        compiler_params=params(20),
        cost_estimate=cost(1),
    )(*aux, mine, theirs, got)


def join_kernel(far, low, high, out):
    own_slot = lax.axis_index("z") // 2
    for i, j in enumerate((1, 0, 3, 2)):
        to, at = slice(i * TILE, (i + 1) * TILE), slice(j * TILE, (j + 1) * TILE)
        both = low[at, :].astype(F32) + high[at, :].astype(F32)
        out[own_slot, to, :] = (far[own_slot, to, :] + both).astype(BF16)
        out[1 - own_slot, to, :] = far[1 - own_slot, to, :].astype(BF16)


def join(far, low, high):
    return pl.pallas_call(
        join_kernel,
        in_specs=[VMEM, VMEM, VMEM],
        out_specs=VMEM,
        out_shape=jax.ShapeDtypeStruct((TILE // BS, N, BS), BF16),
        compiler_params=params(20),
    )(far, low, high)


def finish_kernel(parts, out):
    out[...] = jnp.sum(parts[...].astype(F32), axis=0)


def finish(parts):
    return pl.pallas_call(
        finish_kernel,
        in_specs=[VMEM],
        out_specs=VMEM,
        out_shape=jax.ShapeDtypeStruct((BS // 2, BS), F32),
        compiler_params=params(16),
    )(parts)


def sums_groups():
    def second(core, odd):
        order = row_order(core, odd)
        return order[NB // 2:] + order[:NB // 2]

    return [
        [(z * 2 + core) * 16 + 2 * b + h for z in (odd, odd + 2) for b in second(core, odd) for h in range(2)]
        for odd in range(2)
        for core in range(2)
    ]


def local(aux_ints, density, pattern, block_sizes):
    core = lax.axis_index("c")
    place = jnp.stack([core, lax.rem(lax.axis_index("z"), 2)])

    def swap(array):
        return lax.ppermute(array, "c", [(0, 1), (1, 0)])

    blocks = density.reshape(ROWS, NB // 2, 2, BS).swapaxes(1, 2)
    blocks = jnp.where(core == 0, blocks, blocks[:, ::-1]).reshape(ROWS, N)
    everyone = jnp.broadcast_to(blocks[None], (CHIP_COUNT, ROWS, N))
    mine = lax.all_to_all(everyone, CHIPS, 0, 0).reshape(HALF, N)
    mine, aux = lax.optimization_barrier((mine, prepare(place, block_sizes, pattern, aux_ints)))
    theirs = swap(mine)
    part = first_part(aux[0], mine)
    got = swap(send_sums(False, aux, theirs, part))
    up, down = near_sums(aux, mine, theirs, got)
    low = lax.ppermute(up, "z", [(i, (i + 1) % 4) for i in range(4)])
    high = lax.ppermute(down, "z", [(i, (i - 1) % 4) for i in range(4)])
    got = swap(send_sums(True, aux, theirs, part))
    far = far_sums(aux, mine, theirs, got)
    chip = join(far, low, high)
    chip = chip.reshape(CHIP_COUNT // 2, BS // 2, BS)
    parts = lax.all_to_all(chip, ("z", "c", "x", "y"), 0, 0, axis_index_groups=sums_groups())
    return finish(parts).T


def solution(mesh):
    whole = Mesh(mesh.devices.reshape(4, 2, 4, 4), ("z", "c", "x", "y"))
    everywhere = ("z", "c", "x", "y")
    in_specs = (P(everywhere, None, None), P(everywhere, None), P(everywhere, None, None), P())
    return jax.shard_map(local, mesh=whole, in_specs=in_specs, out_specs=P(("z", "c"), ("x", "y")), check_vma=False)
```
